512 devices in a mesh: ctx: 32 (over y, z_hi, core), resp: 16 (over z_lo, x).
Axes of the slice: x: 4, y: 4, z: 16 (z_hi: 4, z_lo: 4; z = z_hi * 4 + z_lo), core: 2. Of those that a mesh axis runs over, the one named last changes fastest.
Arguments:
- queries: bfloat16 [32, 2048, 1024], P('ctx', 'resp'), may hold values from -4.5 to 4.5
- resp_keys: bfloat16 [32, 2048, 128], P('ctx', 'resp'), may hold values from -4.5 to 4.5
- resp_values: bfloat16 [32, 2048, 128], P('ctx', 'resp'), may hold values from -6 to 6
- prompt_keys: bfloat16 [2048, 128], P('ctx'), may hold values from -4.5 to 4.5
- prompt_values: bfloat16 [2048, 128], P('ctx'), may hold values from -6 to 6
- cotangent: bfloat16 [32, 2048, 1024], P('ctx', 'resp'), may hold values from -6 to 6
- lengths: int32 [32], P('ctx'), may hold values from 256 to 2048, as said below
Outputs:
- attn_out: bfloat16 [32, 2048, 1024], P('ctx', 'resp')
- grad_queries: bfloat16 [32, 2048, 1024], P('ctx', 'resp')
- grad_resp_keys: float32 [32, 2048, 128], P('ctx', 'resp')
- grad_resp_values: float32 [32, 2048, 128], P('ctx', 'resp')
- grad_prompt_keys: float32 [2048, 128], P('ctx')
- grad_prompt_values: float32 [2048, 128], P('ctx')
The draws below stay inside these ranges and needn't reach their ends.
Inputs may be any that keep to these rules, and one draw needn't show every extreme that they name: `lengths`: some response has length 2048 in every draw.
All inputs are finite; a program needn't handle non-finite values.
Results may differ from the reference program's by a relative error of at most 0.0098.
Values may be sent and summed in bfloat16 or wider, within the bound.
No kernel may reach another device: no remote copies, remote signals or barrier semaphores. Data moves between devices by JAX's collectives and lax.ppermute only.
A program may use at most 64 MiB of HBM per device.

```python
import math
import jax
import jax.numpy as jnp
from jax import lax

HD = 128
HG = 8
RESPONSES = 32
LEN = 2048
PROMPT = 2048


def draw_queries(key, part):
    key = jax.random.fold_in(key, 1)
    shape = (RESPONSES, LEN, HG * HD)
    values = jax.random.truncated_normal(key, -4.5, 4.5, shape, jnp.float32)
    return values.astype(jnp.bfloat16)


def draw_prompt_keys(key, part):
    key = jax.random.fold_in(key, 2)
    shape = (PROMPT, HD)
    values = jax.random.truncated_normal(key, -4.5, 4.5, shape, jnp.float32)
    return values.astype(jnp.bfloat16)


def draw_lengths(key, part):
    key = jax.random.fold_in(key, 3)
    drawn = jax.random.randint(key, (RESPONSES,), LEN // 8, LEN + 1, dtype=jnp.int32)
    chosen = jax.random.randint(jax.random.fold_in(key, 4), (), 0, RESPONSES, dtype=jnp.int32)
    return drawn.at[chosen].set(LEN)


def steps_of(stream_key, shape, pieces, smallest, top_value):
    def one(axis_at, shards_of):
        heights = jax.random.uniform(jax.random.fold_in(jax.random.fold_in(stream_key, 6), axis_at), (shards_of,), jnp.float32, smallest / len(pieces), top_value / len(pieces))
        return jnp.repeat(jnp.exp(heights), shape[axis_at] // shards_of).reshape((-1,) + (1,) * (len(shape) - axis_at - 1))

    loudness = one(*pieces[0])
    for cut in pieces[1:]:
        loudness = loudness * one(*cut)
    return loudness


def gaussian(own_key, shape, width, limit, shards=(), kind=jnp.bfloat16):
    values = width * jax.random.normal(own_key, shape, jnp.float32)
    if shards:
        values = values * steps_of(own_key, shape, shards, -0.22, 0.18)
    return jnp.clip(values, -limit, limit).astype(kind)


def setup_inputs(seed: int = 0) -> dict:
    arg_keys = jax.random.split(jax.random.key(seed), 8)
    queries = draw_queries(jax.random.fold_in(arg_keys[7], 71), 0)
    resp_keys = gaussian(arg_keys[1], (RESPONSES, LEN, HD), 1.0, 4.5, ((0, 32), (1, 16)))
    resp_values = gaussian(arg_keys[2], (RESPONSES, LEN, HD), 1.0, 6.0, ((0, 32), (1, 16)))
    prompt_keys = draw_prompt_keys(jax.random.fold_in(arg_keys[7], 71), 0)
    prompt_values = gaussian(arg_keys[4], (PROMPT, HD), 1.0, 6.0, ((0, 32),))
    cotangent = gaussian(arg_keys[5], (RESPONSES, LEN, HG * HD), 1.0, 6.0, ((0, 32), (1, 16)))
    lengths = draw_lengths(jax.random.fold_in(arg_keys[7], 71), 0)
    return dict(queries=queries, resp_keys=resp_keys, resp_values=resp_values, prompt_keys=prompt_keys, prompt_values=prompt_values, cotangent=cotangent, lengths=lengths)


def one_response(query_block, resp_key, resp_value, cot_block, length, prompt_keys, prompt_values):
    count = LEN * HG
    scale = 1.0 / math.sqrt(HD)
    query_rows = query_block.reshape(count, HD)
    keys = jnp.concatenate([prompt_keys, resp_key], 0)
    values = jnp.concatenate([prompt_values, resp_value], 0)
    query_pos = jnp.arange(count, dtype=jnp.int32) // HG
    key_pos = jnp.arange(LEN, dtype=jnp.int32)
    allowed = jnp.concatenate([jnp.ones((count, PROMPT), dtype=bool), key_pos[None, :] <= query_pos[:, None]], 1)
    scores = jnp.dot(query_rows, keys.T, preferred_element_type=jnp.float32) * scale
    scores = jnp.where(allowed, scores, -jnp.inf)
    top = lax.optimization_barrier(jnp.max(scores, 1, keepdims=True))
    lse = top + jnp.log(lax.optimization_barrier(jnp.sum(jnp.exp(scores - top), 1, keepdims=True)))
    weights = jnp.exp(scores - lse)
    probs = weights.astype(jnp.bfloat16)
    valid = (query_pos < length)[:, None]
    full_out = jnp.where(valid, jnp.dot(probs, values, preferred_element_type=jnp.float32), 0.0)
    masked = jnp.where(valid, cot_block.reshape(count, HD), jnp.zeros((), jnp.bfloat16))
    delta = lax.optimization_barrier(jnp.sum(masked.astype(jnp.float32) * full_out, 1, keepdims=True))
    dprobs = jnp.dot(masked, values.T, preferred_element_type=jnp.float32)
    dscores = (weights * (dprobs - delta) * scale).astype(jnp.bfloat16)
    grad_rows = jnp.dot(dscores, keys, preferred_element_type=jnp.float32).astype(jnp.bfloat16)
    grad_keys = jnp.dot(dscores.T, query_rows, preferred_element_type=jnp.float32)
    grad_values = jnp.dot(probs.T, masked, preferred_element_type=jnp.float32)
    attn_block = full_out.astype(jnp.bfloat16).reshape(LEN, HG * HD)
    return (attn_block, grad_rows.reshape(LEN, HG * HD), grad_keys[PROMPT:], grad_values[PROMPT:], grad_keys[:PROMPT], grad_values[:PROMPT])

def reference(queries, resp_keys, resp_values, prompt_keys, prompt_values, cotangent, lengths):

    def single(items):
        return one_response(items[0], items[1], items[2], items[3], items[4], prompt_keys, prompt_values)
    results = lax.map(single, (queries, resp_keys, resp_values, cotangent, lengths))
    grad_prompt_keys = lax.optimization_barrier(jnp.sum(results[4], 0))
    grad_prompt_values = lax.optimization_barrier(jnp.sum(results[5], 0))
    return (results[0], results[1], results[2], results[3], grad_prompt_keys, grad_prompt_values)
```

```python
import math

import jax
import jax.numpy as jnp
from jax import lax
from jax.experimental import pallas as pl
from jax.experimental.pallas import tpu as pltpu
from jax.sharding import PartitionSpec as P

HEAD = 128
HEADS = 8
BLOCK = 128
ROWS = BLOCK * HEADS
CHUNK = 512
PROMPT = 2048
LEN = 2048
WIDE = 2 * HEAD
SCALE = 1.0 / math.sqrt(HEAD)
EXP2_SCALE = SCALE * math.log2(math.e)
MIB = 1024 * 1024

AXES = ("y", "zh", "core", "zl", "x")
CTX = ("y", "zh", "core")
RESP = ("zl", "x")
NEAR = ("y", "core")

F32 = jnp.float32
BF16 = jnp.bfloat16


def load_rows(q_rows, q_ref):
    for h in range(HEADS):
        q_rows[h * BLOCK:(h + 1) * BLOCK, :] = q_ref[:, h * HEAD:(h + 1) * HEAD]


def fold(op, values):
    return op(values.reshape(values.shape[0] // 8, 8, ROWS), 0)


def scores_of(keys, q_rows):
    return lax.dot_general(keys, q_rows[...], (((1,), (1,)), ((), ())), preferred_element_type=F32)


def resp_rows(refs, j):
    rows = pl.ds(pl.multiple_of(j * BLOCK, BLOCK), BLOCK)
    return jnp.concatenate([ref[rows, at:at + HEAD] for ref, at in refs], 0)


def key_refs(r0, r1, r2k, r3):
    return ((r0, 0), (r1, 0), (r2k, 0), (r3, 0))


def value_refs(r0, r1, r2v, r3):
    return ((r0, HEAD), (r1, HEAD), (r2v, 0), (r3, HEAD))


def masked_scores(keys, q_rows, zl, x):
    s = scores_of(keys, q_rows)
    row = lax.broadcasted_iota(jnp.int32, (CHUNK, ROWS), 0)
    key_pos = ((x - row // BLOCK) & 3) * BLOCK + row % BLOCK
    query_pos = x * BLOCK + lax.broadcasted_iota(jnp.int32, (CHUNK, ROWS), 1) % BLOCK
    return jnp.where(key_pos <= query_pos, s, -1e30)


def resp_forward_kernel(place, q_ref, r0, r1, r2k, r2v, r3, top_ref, total_ref, acc_ref, q_rows, s_all):
    keys = key_refs(r0, r1, r2k, r3)
    values = value_refs(r0, r1, r2v, r3)
    zl, x = place[0], place[1]
    load_rows(q_rows, q_ref)

    s = masked_scores(resp_rows(keys, 0), q_rows, zl, x)
    s_all[0:CHUNK, :] = s
    top_ref[...] = fold(jnp.max, s)

    def score_step(j, carry):
        s = scores_of(resp_rows(keys, j), q_rows)
        s_all[pl.ds(pl.multiple_of(j * CHUNK, CHUNK), CHUNK), :] = s
        top_ref[...] = jnp.maximum(top_ref[...], fold(jnp.max, s))
        return carry

    lax.fori_loop(1, zl + 1, score_step, 0)
    peak = jnp.max(top_ref[...], 0, keepdims=True)
    total_ref[...] = jnp.zeros(total_ref.shape, F32)
    acc_ref[...] = jnp.zeros(acc_ref.shape, F32)

    def weight_step(j, carry):
        at = pl.ds(pl.multiple_of(j * CHUNK, CHUNK), CHUNK)
        e = jnp.exp2((s_all[at, :] - peak) * EXP2_SCALE)
        total_ref[...] += fold(jnp.sum, e)
        acc_ref[...] += jnp.dot(resp_rows(values, j).T, e.astype(BF16), preferred_element_type=F32)
        return carry

    lax.fori_loop(0, zl + 1, weight_step, 0)


def prompt_kernel(place, q_ref, c_ref, pkv_ref, rtop_ref, rtotal_ref, racc_ref,
                  out_ref, pg_ref, dq_ref, c_cols, delta_ref, peak_ref,
                  q_rows, c_rows, s_all, e_all, top, total, acc):
    first = (place[0] * 4 + place[1]) * BLOCK
    length = place[2]
    steps = PROMPT // CHUNK
    load_rows(q_rows, q_ref)
    top[...] = rtop_ref[...]

    def rows_of(i):
        return pl.ds(pl.multiple_of(i * CHUNK, CHUNK), CHUNK)

    def score_step(i, carry):
        s = scores_of(pkv_ref[rows_of(i), 0:HEAD], q_rows)
        s_all[rows_of(i), :] = s
        top[...] = jnp.maximum(top[...], fold(jnp.max, s))
        return carry

    lax.fori_loop(0, steps, score_step, 0)
    peak = jnp.max(top[...], 0, keepdims=True)
    peak_ref[...] = peak
    share = jnp.exp2((jnp.max(rtop_ref[...], 0, keepdims=True) - peak) * EXP2_SCALE)
    total[...] = rtotal_ref[...] * share
    acc[...] = racc_ref[...] * share

    def weight_step(i, carry):
        e = jnp.exp2((s_all[rows_of(i), :] - peak) * EXP2_SCALE)
        total[...] += fold(jnp.sum, e)
        e = e.astype(BF16)
        e_all[rows_of(i), :] = e
        acc[...] += jnp.dot(pkv_ref[rows_of(i), HEAD:WIDE].T, e, preferred_element_type=F32)
        return carry

    lax.fori_loop(0, steps, weight_step, 0)
    inverse = 1.0 / jnp.sum(total[...], 0, keepdims=True)

    for h in range(HEADS):
        cols = slice(h * BLOCK, (h + 1) * BLOCK)
        query_pos = first + lax.broadcasted_iota(jnp.int32, (HEAD, BLOCK), 1)
        valid = query_pos < length
        inv = inverse[:, cols]
        out = jnp.where(valid, acc[:, cols] * inv, 0.0)
        out_ref[:, h * HEAD:(h + 1) * HEAD] = out.T.astype(BF16)
        cot = c_ref[:, h * HEAD:(h + 1) * HEAD].astype(F32).T
        cot = jnp.where(valid, cot * inv, 0.0)
        cot16 = cot.astype(BF16)
        c_cols[:, cols] = cot16
        c_rows[cols, :] = cot16.astype(F32).T.astype(BF16)
        delta_ref[:, cols] = jnp.sum(cot16.astype(F32) * out, 0, keepdims=True)
    delta = delta_ref[...]
    dq_ref[...] = jnp.zeros(dq_ref.shape, F32)

    def grad_step(i, carry):
        keys = pkv_ref[rows_of(i), 0:HEAD]
        values = pkv_ref[rows_of(i), HEAD:WIDE]
        e = e_all[rows_of(i), :]
        dp = jnp.dot(values, c_cols[...], preferred_element_type=F32)
        ds = (dp - delta).astype(BF16) * e
        dq_ref[...] += jnp.dot(keys.T, ds, preferred_element_type=F32)
        dk = jnp.dot(ds, q_rows[...], preferred_element_type=F32) * SCALE
        dv = jnp.dot(e, c_rows[...], preferred_element_type=F32)
        pg_ref[rows_of(i), 0:HEAD] = dk.astype(BF16)
        pg_ref[rows_of(i), HEAD:WIDE] = dv.astype(BF16)
        return carry

    lax.fori_loop(0, steps, grad_step, 0)


def resp_backward_kernel(place, q_ref, r0, r1, r2k, r2v, r3, c_cols, delta_ref, peak_ref, dqp_ref,
                         dq_ref, rg_ref, q_rows, c_rows, acc):
    key_at = key_refs(r0, r1, r2k, r3)
    value_at = value_refs(r0, r1, r2v, r3)
    zl, x = place[0], place[1]
    load_rows(q_rows, q_ref)
    for h in range(HEADS):
        cols = slice(h * BLOCK, (h + 1) * BLOCK)
        c_rows[cols, :] = c_cols[:, cols].astype(F32).T.astype(BF16)
    acc[...] = dqp_ref[...]
    delta = delta_ref[...]
    peak = peak_ref[...]

    def grad_step(j, keys, s):
        e = jnp.exp2((s - peak) * EXP2_SCALE).astype(BF16)
        dp = jnp.dot(resp_rows(value_at, j), c_cols[...], preferred_element_type=F32)
        ds = (dp - delta).astype(BF16) * e
        acc[...] += jnp.dot(keys.T, ds, preferred_element_type=F32)
        dk = (jnp.dot(ds, q_rows[...], preferred_element_type=F32) * SCALE).astype(BF16)
        dv = jnp.dot(e, c_rows[...], preferred_element_type=F32).astype(BF16)
        at = pl.ds(pl.multiple_of(j * BLOCK, BLOCK), BLOCK)
        for i in range(4):
            rows = slice(i * BLOCK, (i + 1) * BLOCK)
            rg_ref[(4 - i) % 4, at, 0:HEAD] = dk[rows]
            rg_ref[(4 - i) % 4, at, HEAD:WIDE] = dv[rows]

    keys = resp_rows(key_at, 0)
    grad_step(0, keys, masked_scores(keys, q_rows, zl, x))

    def full_step(j, carry):
        keys = resp_rows(key_at, j)
        grad_step(j, keys, scores_of(keys, q_rows))
        return carry

    lax.fori_loop(1, zl + 1, full_step, 0)
    for h in range(HEADS):
        dq = acc[:, h * BLOCK:(h + 1) * BLOCK] * SCALE
        dq_ref[:, h * HEAD:(h + 1) * HEAD] = dq.T.astype(BF16)


def call(kernel, args, outs, scratch, matmuls, keys):
    smem = pl.BlockSpec(memory_space=pltpu.SMEM)
    vmem = pl.BlockSpec(memory_space=pltpu.VMEM)
    return pl.pallas_call(
        kernel,
        out_shape=tuple(jax.ShapeDtypeStruct(shape, dtype) for shape, dtype in outs),
        in_specs=[smem] + [vmem] * (len(args) - 1),
        out_specs=(vmem,) * len(outs),
        scratch_shapes=[pltpu.VMEM(shape, dtype) for shape, dtype in scratch],
        compiler_params=pltpu.CompilerParams(vmem_limit_bytes=32 * MIB),
        cost_estimate=pl.CostEstimate(
            flops=2 * matmuls * ROWS * keys * HEAD,
            bytes_accessed=6 * MIB,
            transcendentals=ROWS * keys,
        ),
    )(*args)


def exchange(blocks, axes):
    return lax.all_to_all(blocks, axes, 0, 0, tiled=True)


def gather(own, axes, count):
    return exchange(jnp.broadcast_to(own[None], (count,) + own.shape), axes)


def around_x(block, shift):
    return lax.ppermute(block, "x", [(x, (x + shift) % 4) for x in range(4)])


def along_zl(block, shift):
    return lax.ppermute(block, "zl", [(z, z + shift) for z in range(4) if 0 <= z + shift < 4])


def swap_zl(block, bit):
    return lax.ppermute(block, "zl", [(z, z ^ bit) for z in range(4)])


def total_of(parts):
    terms = [parts[i].astype(F32) for i in range(len(parts))]
    while len(terms) > 1:
        terms = [terms[i] + terms[i + 1] for i in range(0, len(terms), 2)]
    return terms[0]


def per_device(queries, resp_keys, resp_values, prompt_keys, prompt_values, cotangent, lengths):
    place = jnp.stack([lax.axis_index("zl"), lax.axis_index("x"), lengths[0]]).astype(jnp.int32)
    queries = queries[0]
    cotangent = cotangent[0]

    own_prompt = jnp.concatenate([prompt_keys, prompt_values], 1)
    own_resp = jnp.concatenate([resp_keys[0], resp_values[0]], 1)
    far = gather(own_prompt, "zh", 4).reshape(PROMPT // 8, WIDE)
    below = [along_zl(own_resp, k) for k in (1, 2, 3)]
    far, *below = lax.optimization_barrier((far, *below))

    pkv = gather(far, NEAR, 8).reshape(PROMPT, WIDE)
    r0 = jnp.concatenate([own_resp] + below, 0)
    r1 = around_x(r0, 1)
    r3 = around_x(r0, 3)
    r2k = around_x(r1[:, :HEAD], 1)
    r2v = around_x(r3[:, HEAD:], 3)
    rkv = [r0, r1, r2k, r2v, r3]

    rtop, rtotal, racc = call(
        resp_forward_kernel,
        [place, queries] + rkv,
        [((8, ROWS), F32), ((8, ROWS), F32), ((HEAD, ROWS), F32)],
        [((ROWS, HEAD), BF16), ((LEN, ROWS), F32)],
        2,
        LEN,
    )
    out, pgrad, dq_prompt, cols, delta, peak = call(
        prompt_kernel,
        [place, queries, cotangent, pkv, rtop, rtotal, racc],
        [((BLOCK, ROWS), BF16), ((PROMPT, WIDE), BF16), ((HEAD, ROWS), F32), ((HEAD, ROWS), BF16),
         ((1, ROWS), F32), ((1, ROWS), F32)],
        [((ROWS, HEAD), BF16), ((ROWS, HEAD), BF16), ((PROMPT, ROWS), F32), ((PROMPT, ROWS), BF16),
         ((8, ROWS), F32), ((8, ROWS), F32), ((HEAD, ROWS), F32)],
        6,
        PROMPT,
    )
    dq, rgrad = call(
        resp_backward_kernel,
        [place, queries] + rkv + [cols, delta, peak, dq_prompt],
        [((BLOCK, ROWS), BF16), ((4, LEN // 4, WIDE), BF16)],
        [((ROWS, HEAD), BF16), ((ROWS, HEAD), BF16), ((HEAD, ROWS), F32)],
        5,
        LEN,
    )

    near, _ = lax.optimization_barrier((exchange(pgrad.reshape(8, PROMPT // 8, WIDE), NEAR), rgrad))
    part = total_of(near).astype(BF16)
    part = total_of(exchange(part.reshape(4, PROMPT // 32, WIDE), "zh")).astype(BF16)

    column = total_of([rgrad[0]] + [around_x(rgrad[k], k) for k in (1, 2, 3)])
    sent = column.astype(BF16)
    down = [along_zl(sent[k * BLOCK:(k + 1) * BLOCK], -k) for k in (1, 2, 3)]
    grad_resp = total_of([column[:BLOCK]] + down)

    ring = [part] + [around_x(part, k) for k in (1, 2, 3)]
    part = total_of([ring[0], ring[2], ring[1], ring[3]]).astype(BF16)
    part = total_of([part, swap_zl(part, 1)]).astype(BF16)
    grad_prompt = total_of([part, swap_zl(part, 2)])
    return (
        out[None],
        dq[None],
        grad_resp[None, :, :HEAD],
        grad_resp[None, :, HEAD:],
        grad_prompt[:, :HEAD],
        grad_prompt[:, HEAD:],
    )


def solution(mesh):
    fine = jax.sharding.Mesh(mesh.devices.reshape(4, 4, 2, 4, 4), AXES)
    rows = P(CTX, RESP, None)
    return jax.shard_map(
        per_device,
        mesh=fine,
        in_specs=(rows, rows, rows, P(CTX, None), P(CTX, None), rows, P(CTX)),
        out_specs=(rows, rows, rows, rows, P(CTX, None), P(CTX, None)),
        check_vma=False,
    )
```

```python
import math

import jax
import jax.numpy as jnp
from jax import lax
from jax.experimental import pallas as pl
from jax.experimental.pallas import tpu as pltpu
from jax.sharding import PartitionSpec as P

HEAD = 128
HEADS = 8
BLOCK = 128
ROWS = BLOCK * HEADS
CHUNK = 512
PROMPT = 2048
LEN = 2048
WIDE = 2 * HEAD
SCALE = 1.0 / math.sqrt(HEAD)
EXP2_SCALE = SCALE * math.log2(math.e)
MIB = 1024 * 1024

AXES = ("y", "zh", "core", "zl", "x")
CTX = ("y", "zh", "core")
RESP = ("zl", "x")
NEAR = ("y", "core")

F32 = jnp.float32
BF16 = jnp.bfloat16


def load_rows(q_rows, q_ref):
    for h in range(HEADS):
        q_rows[h * BLOCK:(h + 1) * BLOCK, :] = q_ref[:, h * HEAD:(h + 1) * HEAD]


def fold(op, values):
    return op(values.reshape(values.shape[0] // 8, 8, ROWS), 0)


def scores_of(keys, q_rows):
    return lax.dot_general(keys, q_rows[...], (((1,), (1,)), ((), ())), preferred_element_type=F32)


def resp_rows(refs, j, at):
    rows = pl.ds(pl.multiple_of(j * BLOCK, BLOCK), BLOCK)
    return jnp.concatenate([ref[rows, at:at + HEAD] for ref in refs], 0)


def chunk_at(i):
    return pl.ds(pl.multiple_of(i * CHUNK, CHUNK), CHUNK)


def masked_scores(keys, q_rows, x):
    s = scores_of(keys, q_rows)
    row = lax.broadcasted_iota(jnp.int32, (CHUNK, ROWS), 0)
    key_pos = ((x - row // BLOCK) & 3) * BLOCK + row % BLOCK
    query_pos = x * BLOCK + lax.broadcasted_iota(jnp.int32, (CHUNK, ROWS), 1) % BLOCK
    return jnp.where(key_pos <= query_pos, s, -1e30)


def prompt_forward_kernel(q_ref, pkv_ref, e_ref, top_ref, total_ref, acc_ref, q_rows, s_all):
    load_rows(q_rows, q_ref)
    top_ref[...] = jnp.full(top_ref.shape, -1e30, F32)

    def score_step(i, carry):
        s = scores_of(pkv_ref[chunk_at(i), 0:HEAD], q_rows)
        s_all[chunk_at(i), :] = s
        top_ref[...] = jnp.maximum(top_ref[...], fold(jnp.max, s))
        return carry

    lax.fori_loop(0, PROMPT // CHUNK, score_step, 0)
    peak = jnp.max(top_ref[...], 0, keepdims=True)
    total_ref[...] = jnp.zeros(total_ref.shape, F32)
    acc_ref[...] = jnp.zeros(acc_ref.shape, F32)

    def weight_step(i, carry):
        e = jnp.exp2((s_all[chunk_at(i), :] - peak) * EXP2_SCALE)
        total_ref[...] += fold(jnp.sum, e)
        e = e.astype(BF16)
        e_ref[chunk_at(i), :] = e
        acc_ref[...] += jnp.dot(pkv_ref[chunk_at(i), HEAD:WIDE].T, e, preferred_element_type=F32)
        return carry

    lax.fori_loop(0, PROMPT // CHUNK, weight_step, 0)


def middle_kernel(place, q_ref, c_ref, pkv_ref, r0, r1, r2, r3, e_ref, ptop_ref, ptotal_ref, pacc_ref,
                  out_ref, pg_ref, dq_ref, cols_ref, delta_ref, peak_ref,
                  q_rows, c_rows, c_cols, pdelta, s_all, top, total, acc):
    refs = (r0, r1, r2, r3)
    zl, x, length = place[0], place[1], place[2]
    first = (zl * 4 + x) * BLOCK
    load_rows(q_rows, q_ref)

    s = masked_scores(resp_rows(refs, 0, 0), q_rows, x)
    s_all[0:CHUNK, :] = s
    top[...] = jnp.maximum(ptop_ref[...], fold(jnp.max, s))

    def score_step(j, carry):
        s = scores_of(resp_rows(refs, j, 0), q_rows)
        s_all[chunk_at(j), :] = s
        top[...] = jnp.maximum(top[...], fold(jnp.max, s))
        return carry

    lax.fori_loop(1, zl + 1, score_step, 0)
    peak = jnp.max(top[...], 0, keepdims=True)
    peak_ref[...] = peak
    share = jnp.exp2((jnp.max(ptop_ref[...], 0, keepdims=True) - peak) * EXP2_SCALE)
    total[...] = ptotal_ref[...] * share
    acc[...] = pacc_ref[...] * share

    def weight_step(j, carry):
        e = jnp.exp2((s_all[chunk_at(j), :] - peak) * EXP2_SCALE)
        total[...] += fold(jnp.sum, e)
        acc[...] += jnp.dot(resp_rows(refs, j, HEAD).T, e.astype(BF16), preferred_element_type=F32)
        return carry

    lax.fori_loop(0, zl + 1, weight_step, 0)
    inverse = 1.0 / jnp.sum(total[...], 0, keepdims=True)

    for h in range(HEADS):
        cols = slice(h * BLOCK, (h + 1) * BLOCK)
        query_pos = first + lax.broadcasted_iota(jnp.int32, (HEAD, BLOCK), 1)
        valid = query_pos < length
        inv = inverse[:, cols]
        out = jnp.where(valid, acc[:, cols] * inv, 0.0)
        out_ref[:, h * HEAD:(h + 1) * HEAD] = out.T.astype(BF16)
        cot = c_ref[:, h * HEAD:(h + 1) * HEAD].astype(F32).T
        cot = jnp.where(valid, cot * inv, 0.0)
        cot16 = cot.astype(BF16)
        cols_ref[:, cols] = cot16
        delta_ref[:, cols] = jnp.sum(cot16.astype(F32) * out, 0, keepdims=True)
        cot16 = (cot * share[:, cols]).astype(BF16)
        c_cols[:, cols] = cot16
        c_rows[cols, :] = cot16.astype(F32).T.astype(BF16)
        pdelta[:, cols] = jnp.sum(cot16.astype(F32) * out, 0, keepdims=True)
    delta = pdelta[...]
    dq_ref[...] = jnp.zeros(dq_ref.shape, F32)

    def grad_step(i, carry):
        keys = pkv_ref[chunk_at(i), 0:HEAD]
        values = pkv_ref[chunk_at(i), HEAD:WIDE]
        e = e_ref[chunk_at(i), :]
        dp = jnp.dot(values, c_cols[...], preferred_element_type=F32)
        ds = (dp - delta).astype(BF16) * e
        dq_ref[...] += jnp.dot(keys.T, ds, preferred_element_type=F32)
        dk = jnp.dot(ds, q_rows[...], preferred_element_type=F32) * SCALE
        dv = jnp.dot(e, c_rows[...], preferred_element_type=F32)
        pg_ref[chunk_at(i), 0:HEAD] = dk.astype(BF16)
        pg_ref[chunk_at(i), HEAD:WIDE] = dv.astype(BF16)
        return carry

    lax.fori_loop(0, PROMPT // CHUNK, grad_step, 0)


def resp_backward_kernel(place, q_ref, r0, r1, r2, r3, c_cols, delta_ref, peak_ref, dqp_ref,
                         dq_ref, rg_ref, q_rows, c_rows, acc):
    refs = (r0, r1, r2, r3)
    zl, x = place[0], place[1]
    load_rows(q_rows, q_ref)
    for h in range(HEADS):
        cols = slice(h * BLOCK, (h + 1) * BLOCK)
        c_rows[cols, :] = c_cols[:, cols].astype(F32).T.astype(BF16)
    acc[...] = dqp_ref[...]
    delta = delta_ref[...]
    peak = peak_ref[...]

    def grad_step(j, keys, s):
        e = jnp.exp2((s - peak) * EXP2_SCALE).astype(BF16)
        dp = jnp.dot(resp_rows(refs, j, HEAD), c_cols[...], preferred_element_type=F32)
        ds = (dp - delta).astype(BF16) * e
        acc[...] += jnp.dot(keys.T, ds, preferred_element_type=F32)
        dk = (jnp.dot(ds, q_rows[...], preferred_element_type=F32) * SCALE).astype(BF16)
        dv = jnp.dot(e, c_rows[...], preferred_element_type=F32).astype(BF16)
        at = pl.ds(pl.multiple_of(j * BLOCK, BLOCK), BLOCK)
        for i in range(4):
            rows = slice(i * BLOCK, (i + 1) * BLOCK)
            rg_ref[(4 - i) % 4, at, 0:HEAD] = dk[rows]
            rg_ref[(4 - i) % 4, at, HEAD:WIDE] = dv[rows]

    keys = resp_rows(refs, 0, 0)
    grad_step(0, keys, masked_scores(keys, q_rows, x))

    def full_step(j, carry):
        keys = resp_rows(refs, j, 0)
        grad_step(j, keys, scores_of(keys, q_rows))
        return carry

    lax.fori_loop(1, zl + 1, full_step, 0)
    for h in range(HEADS):
        dq = acc[:, h * BLOCK:(h + 1) * BLOCK] * SCALE
        dq_ref[:, h * HEAD:(h + 1) * HEAD] = dq.T.astype(BF16)


def call(kernel, place, args, outs, scratch, matmuls, keys):
    smem = pl.BlockSpec(memory_space=pltpu.SMEM)
    vmem = pl.BlockSpec(memory_space=pltpu.VMEM)
    return pl.pallas_call(
        kernel,
        out_shape=tuple(jax.ShapeDtypeStruct(shape, dtype) for shape, dtype in outs),
        in_specs=[smem] * len(place) + [vmem] * len(args),
        out_specs=(vmem,) * len(outs),
        scratch_shapes=[pltpu.VMEM(shape, dtype) for shape, dtype in scratch],
        compiler_params=pltpu.CompilerParams(vmem_limit_bytes=32 * MIB),
        cost_estimate=pl.CostEstimate(
            flops=2 * matmuls * ROWS * keys * HEAD,
            bytes_accessed=6 * MIB,
            transcendentals=ROWS * keys,
        ),
    )(*place, *args)


def exchange(blocks, axes):
    return lax.all_to_all(blocks, axes, 0, 0, tiled=True)


def gather(own, axes, count):
    return exchange(jnp.broadcast_to(own[None], (count,) + own.shape), axes)


def around_x(block, shift):
    return lax.ppermute(block, "x", [(x, (x + shift) % 4) for x in range(4)])


def along_zl(block, shift):
    return lax.ppermute(block, "zl", [(z, z + shift) for z in range(4) if 0 <= z + shift < 4])


def swap_zl(block, bit):
    return lax.ppermute(block, "zl", [(z, z ^ bit) for z in range(4)])


def total_of(parts):
    terms = [parts[i].astype(F32) for i in range(len(parts))]
    while len(terms) > 1:
        terms = [terms[i] + terms[i + 1] for i in range(0, len(terms), 2)]
    return terms[0]


def per_device(queries, resp_keys, resp_values, prompt_keys, prompt_values, cotangent, lengths):
    place = jnp.stack([lax.axis_index("zl"), lax.axis_index("x"), lengths[0]]).astype(jnp.int32)
    queries = queries[0]
    cotangent = cotangent[0]

    own_prompt = jnp.concatenate([prompt_keys, prompt_values], 1)
    own_resp = jnp.concatenate([resp_keys[0], resp_values[0]], 1)
    far = gather(own_prompt, "zh", 4).reshape(PROMPT // 8, WIDE)
    below = [along_zl(own_resp, k) for k in (1, 2, 3)]
    far, *below = lax.optimization_barrier((far, *below))

    pkv = gather(far, NEAR, 8).reshape(PROMPT, WIDE)
    column = jnp.concatenate([own_resp] + below, 0)
    rkv = [column] + [around_x(column, k) for k in (1, 2, 3)]

    forward = call(
        prompt_forward_kernel,
        [],
        [queries, pkv],
        [((PROMPT, ROWS), BF16), ((8, ROWS), F32), ((8, ROWS), F32), ((HEAD, ROWS), F32)],
        [((ROWS, HEAD), BF16), ((PROMPT, ROWS), F32)],
        2,
        PROMPT,
    )
    out, pgrad, dq_prompt, cols, delta, peak = call(
        middle_kernel,
        [place],
        [queries, cotangent, pkv] + rkv + list(forward),
        [((BLOCK, ROWS), BF16), ((PROMPT, WIDE), BF16), ((HEAD, ROWS), F32), ((HEAD, ROWS), BF16),
         ((1, ROWS), F32), ((1, ROWS), F32)],
        [((ROWS, HEAD), BF16), ((ROWS, HEAD), BF16), ((HEAD, ROWS), BF16), ((1, ROWS), F32),
         ((LEN, ROWS), F32), ((8, ROWS), F32), ((8, ROWS), F32), ((HEAD, ROWS), F32)],
        6,
        PROMPT,
    )
    dq, rgrad = call(
        resp_backward_kernel,
        [place],
        [queries] + rkv + [cols, delta, peak, dq_prompt],
        [((BLOCK, ROWS), BF16), ((4, LEN // 4, WIDE), BF16)],
        [((ROWS, HEAD), BF16), ((ROWS, HEAD), BF16), ((HEAD, ROWS), F32)],
        5,
        LEN,
    )

    near, _ = lax.optimization_barrier((exchange(pgrad.reshape(8, PROMPT // 8, WIDE), NEAR), rgrad))
    part = total_of(near).astype(BF16)
    part = exchange(part.reshape(4, PROMPT // 32, WIDE), "zh")

    column = total_of([rgrad[0]] + [around_x(rgrad[k], k) for k in (1, 2, 3)])
    sent = column.astype(BF16)
    down = [along_zl(sent[k * BLOCK:(k + 1) * BLOCK], -k) for k in (1, 2, 3)]
    part, *down = lax.optimization_barrier((part, *down))
    grad_resp = total_of([column[:BLOCK]] + down)

    part = total_of(part).astype(BF16)
    ring = [part] + [around_x(part, k) for k in (1, 2, 3)]
    part = total_of([ring[0], ring[2], ring[1], ring[3]]).astype(BF16)
    part = total_of([part, swap_zl(part, 1)]).astype(BF16)
    grad_prompt = total_of([part, swap_zl(part, 2)])
    return (
        out[None],
        dq[None],
        grad_resp[None, :, :HEAD],
        grad_resp[None, :, HEAD:],
        grad_prompt[:, :HEAD],
        grad_prompt[:, HEAD:],
    )


def solution(mesh):
    fine = jax.sharding.Mesh(mesh.devices.reshape(4, 4, 2, 4, 4), AXES)
    rows = P(CTX, RESP, None)
    return jax.shard_map(
        per_device,
        mesh=fine,
        in_specs=(rows, rows, rows, P(CTX, None), P(CTX, None), rows, P(CTX)),
        out_specs=(rows, rows, rows, rows, P(CTX, None), P(CTX, None)),
        check_vma=False,
    )
```

```python
import math

import jax
import jax.numpy as jnp
from jax import lax
from jax.experimental import pallas as pl
from jax.experimental.pallas import tpu as pltpu
from jax.sharding import PartitionSpec as P

HEAD = 128
HEADS = 8
BLOCK = 128
ROWS = BLOCK * HEADS
CHUNK = 512
PROMPT = 2048
LEN = 2048
PIECE = 16
WIDE = 2 * HEAD
SCALE = 1.0 / math.sqrt(HEAD)
EXP2_SCALE = SCALE * math.log2(math.e)
MIB = 1024 * 1024

AXES = ("y", "zh", "core", "zl", "x")
CTX = ("y", "zh", "core")
RESP = ("zl", "x")
NEAR = ("y", "core")

F32 = jnp.float32
BF16 = jnp.bfloat16


def load_rows(q_rows, q_ref):
    for h in range(HEADS):
        q_rows[h * BLOCK:(h + 1) * BLOCK, :] = q_ref[:, h * HEAD:(h + 1) * HEAD]


def fold(op, values):
    return op(values.reshape(values.shape[0] // 8, 8, ROWS), 0)


def scores_of(keys, q_rows):
    return lax.dot_general(keys, q_rows[...], (((1,), (1,)), ((), ())), preferred_element_type=F32)


def resp_rows(refs, j, at):
    rows = pl.ds(pl.multiple_of(j * BLOCK, BLOCK), BLOCK)
    return jnp.concatenate([ref[rows, at:at + HEAD] for ref in refs], 0)


def chunk_at(i):
    return pl.ds(pl.multiple_of(i * CHUNK, CHUNK), CHUNK)


def bias_of(key_pos, x):
    query_pos = x * BLOCK + lax.broadcasted_iota(jnp.int32, (CHUNK, BLOCK), 1)
    return jnp.where(key_pos <= query_pos, 0.0, -1e30).astype(F32)


def chunk_rows():
    row = lax.broadcasted_iota(jnp.int32, (CHUNK, BLOCK), 0)
    return row // BLOCK, row % BLOCK


def level_bias(x):
    slot, row = chunk_rows()
    return bias_of(((x - slot) & 3) * BLOCK + row, x)


def column_bias(zl, x, i):
    slot, row = chunk_rows()
    key_pos = (((x - i) & 3) - 4 * slot) * BLOCK + row
    return bias_of(jnp.where(slot <= zl, key_pos, LEN), x)


def biased(s, bias):
    return s + jnp.concatenate([bias] * HEADS, 1)


def column_scores(columns, zl, x, q_rows, s_all, start, top):
    for n, (ref, i) in enumerate(columns):
        s = biased(scores_of(ref[:, 0:HEAD], q_rows), column_bias(zl, x, i))
        s_all[start + n * CHUNK:start + (n + 1) * CHUNK, :] = s
        top[...] = jnp.maximum(top[...], fold(jnp.max, s))


def column_weights(columns, peak, s_all, start, total, acc):
    for n, (ref, i) in enumerate(columns):
        e = jnp.exp2((s_all[start + n * CHUNK:start + (n + 1) * CHUNK, :] - peak) * EXP2_SCALE)
        total[...] += fold(jnp.sum, e)
        acc[...] += jnp.dot(ref[:, HEAD:WIDE].T, e.astype(BF16), preferred_element_type=F32)


def prompt_forward_kernel(place, q_ref, pkv_ref, r0, r3, e_ref, top_ref, total_ref, acc_ref, q_rows, s_all):
    zl, x = place[0], place[1]
    columns = ((r0, 0), (r3, 3))
    load_rows(q_rows, q_ref)
    top_ref[...] = jnp.full(top_ref.shape, -1e30, F32)

    def score_step(i, carry):
        s = scores_of(pkv_ref[chunk_at(i), 0:HEAD], q_rows)
        s_all[chunk_at(i), :] = s
        top_ref[...] = jnp.maximum(top_ref[...], fold(jnp.max, s))
        return carry

    lax.fori_loop(0, PROMPT // CHUNK, score_step, 0)
    column_scores(columns, zl, x, q_rows, s_all, PROMPT, top_ref)
    peak = jnp.max(top_ref[...], 0, keepdims=True)
    total_ref[...] = jnp.zeros(total_ref.shape, F32)
    acc_ref[...] = jnp.zeros(acc_ref.shape, F32)

    def weight_step(i, carry):
        e = jnp.exp2((s_all[chunk_at(i), :] - peak) * EXP2_SCALE)
        total_ref[...] += fold(jnp.sum, e)
        e = e.astype(BF16)
        e_ref[chunk_at(i), :] = e
        acc_ref[...] += jnp.dot(pkv_ref[chunk_at(i), HEAD:WIDE].T, e, preferred_element_type=F32)
        return carry

    lax.fori_loop(0, PROMPT // CHUNK, weight_step, 0)
    column_weights(columns, peak, s_all, PROMPT, total_ref, acc_ref)


def middle_kernel(place, q_ref, c_ref, pkv_ref, r1, r2, e_ref, ptop_ref, ptotal_ref, pacc_ref,
                  out_ref, pg_ref, dq_ref, cols_ref, delta_ref, peak_ref,
                  q_rows, c_rows, c_cols, pdelta, s_all, top, total, acc):
    columns = ((r1, 1), (r2, 2))
    zl, x, length = place[0], place[1], place[2]
    first = (zl * 4 + x) * BLOCK
    load_rows(q_rows, q_ref)

    top[...] = ptop_ref[...]
    column_scores(columns, zl, x, q_rows, s_all, 0, top)
    peak = jnp.max(top[...], 0, keepdims=True)
    peak_ref[...] = peak
    share = jnp.exp2((jnp.max(ptop_ref[...], 0, keepdims=True) - peak) * EXP2_SCALE)
    total[...] = ptotal_ref[...] * share
    acc[...] = pacc_ref[...] * share
    column_weights(columns, peak, s_all, 0, total, acc)
    inverse = 1.0 / jnp.sum(total[...], 0, keepdims=True)

    for h in range(HEADS):
        cols = slice(h * BLOCK, (h + 1) * BLOCK)
        query_pos = first + lax.broadcasted_iota(jnp.int32, (HEAD, BLOCK), 1)
        valid = query_pos < length
        inv = inverse[:, cols]
        out = jnp.where(valid, acc[:, cols] * inv, 0.0)
        out_ref[:, h * HEAD:(h + 1) * HEAD] = out.T.astype(BF16)
        cot = c_ref[:, h * HEAD:(h + 1) * HEAD].astype(F32).T
        cot = jnp.where(valid, cot * inv, 0.0)
        cot16 = cot.astype(BF16)
        cols_ref[:, cols] = cot16
        delta_ref[:, cols] = jnp.sum(cot16.astype(F32) * out, 0, keepdims=True)
        cot16 = (cot * share[:, cols]).astype(BF16)
        c_cols[:, cols] = cot16
        c_rows[cols, :] = cot16.astype(F32).T.astype(BF16)
        pdelta[:, cols] = jnp.sum(cot16.astype(F32) * out, 0, keepdims=True)
    delta = pdelta[...]
    dq_ref[...] = jnp.zeros(dq_ref.shape, F32)

    def grad_step(i, carry):
        keys = pkv_ref[chunk_at(i), 0:HEAD]
        values = pkv_ref[chunk_at(i), HEAD:WIDE]
        e = e_ref[chunk_at(i), :]
        dp = jnp.dot(values, c_cols[...], preferred_element_type=F32)
        ds = (dp - delta).astype(BF16) * e
        dq_ref[...] += jnp.dot(keys.T, ds, preferred_element_type=F32)
        dk = jnp.dot(ds, q_rows[...], preferred_element_type=F32) * SCALE
        dv = jnp.dot(e, c_rows[...], preferred_element_type=F32)
        pg_ref[chunk_at(i), 0:HEAD] = dk.astype(BF16)
        pg_ref[chunk_at(i), HEAD:WIDE] = dv.astype(BF16)
        return carry

    lax.fori_loop(0, PROMPT // CHUNK, grad_step, 0)


def resp_backward_kernel(place, q_ref, r0, r1, r2, r3, c_cols, delta_ref, peak_ref, dqp_ref,
                         dq_ref, rg_ref, q_rows, c_rows, acc):
    refs = (r0, r1, r2, r3)
    zl, x = place[0], place[1]
    load_rows(q_rows, q_ref)
    for h in range(HEADS):
        cols = slice(h * BLOCK, (h + 1) * BLOCK)
        c_rows[cols, :] = c_cols[:, cols].astype(F32).T.astype(BF16)
    acc[...] = dqp_ref[...]
    delta = delta_ref[...]
    peak = peak_ref[...]

    def grad_step(j, keys, s):
        e = jnp.exp2((s - peak) * EXP2_SCALE).astype(BF16)
        dp = jnp.dot(resp_rows(refs, j, HEAD), c_cols[...], preferred_element_type=F32)
        ds = (dp - delta).astype(BF16) * e
        acc[...] += jnp.dot(keys.T, ds, preferred_element_type=F32)
        dk = (jnp.dot(ds, q_rows[...], preferred_element_type=F32) * SCALE).astype(BF16)
        dv = jnp.dot(e, c_rows[...], preferred_element_type=F32).astype(BF16)
        at = pl.ds(pl.multiple_of(j * BLOCK, BLOCK), BLOCK)
        for i in range(4):
            rows = slice(i * BLOCK, (i + 1) * BLOCK)
            rg_ref[(4 - i) % 4, at, 0:HEAD] = dk[rows]
            rg_ref[(4 - i) % 4, at, HEAD:WIDE] = dv[rows]

    keys = resp_rows(refs, 0, 0)
    grad_step(0, keys, biased(scores_of(keys, q_rows), level_bias(x)))

    def full_step(j, carry):
        keys = resp_rows(refs, j, 0)
        grad_step(j, keys, scores_of(keys, q_rows))
        return carry

    lax.fori_loop(1, zl + 1, full_step, 0)
    for h in range(HEADS):
        dq = acc[:, h * BLOCK:(h + 1) * BLOCK] * SCALE
        dq_ref[:, h * HEAD:(h + 1) * HEAD] = dq.T.astype(BF16)


def call(kernel, place, args, outs, scratch, matmuls, keys):
    smem = pl.BlockSpec(memory_space=pltpu.SMEM)
    vmem = pl.BlockSpec(memory_space=pltpu.VMEM)
    return pl.pallas_call(
        kernel,
        out_shape=tuple(jax.ShapeDtypeStruct(shape, dtype) for shape, dtype in outs),
        in_specs=[smem] * len(place) + [vmem] * len(args),
        out_specs=(vmem,) * len(outs),
        scratch_shapes=[pltpu.VMEM(shape, dtype) for shape, dtype in scratch],
        compiler_params=pltpu.CompilerParams(vmem_limit_bytes=32 * MIB),
        cost_estimate=pl.CostEstimate(
            flops=2 * matmuls * ROWS * keys * HEAD,
            bytes_accessed=6 * MIB,
            transcendentals=ROWS * keys,
        ),
    )(*place, *args)


def exchange(blocks, axes):
    return lax.all_to_all(blocks, axes, 0, 0, tiled=True)


def gather(own, axes, count):
    return exchange(jnp.broadcast_to(own[None], (count,) + own.shape), axes)


def around_x(block, shift):
    return lax.ppermute(block, "x", [(x, (x + shift) % 4) for x in range(4)])


def along_zl(block, shift):
    return lax.ppermute(block, "zl", [(z, z + shift) for z in range(4) if 0 <= z + shift < 4])


def total_of(parts):
    terms = [parts[i].astype(F32) for i in range(len(parts))]
    while len(terms) > 1:
        terms = [terms[i] + terms[i + 1] for i in range(0, len(terms), 2)]
    return terms[0]


def per_device(queries, resp_keys, resp_values, prompt_keys, prompt_values, cotangent, lengths):
    place = jnp.stack([lax.axis_index("zl"), lax.axis_index("x"), lengths[0]]).astype(jnp.int32)
    queries = queries[0]
    cotangent = cotangent[0]

    own_prompt = jnp.concatenate([prompt_keys, prompt_values], 1)
    own_resp = jnp.concatenate([resp_keys[0], resp_values[0]], 1)
    far = gather(own_prompt, "zh", 4).reshape(PROMPT // 8, WIDE)
    below = [along_zl(own_resp, k) for k in (1, 2, 3)]
    far, *below = lax.optimization_barrier((far, *below))

    pkv = gather(far, NEAR, 8).reshape(PROMPT, WIDE)
    column = jnp.concatenate([own_resp] + below, 0)
    rkv = [column] + [around_x(column, k) for k in (1, 2, 3)]

    forward = call(
        prompt_forward_kernel,
        [place],
        [queries, pkv, rkv[0], rkv[3]],
        [((PROMPT, ROWS), BF16), ((8, ROWS), F32), ((8, ROWS), F32), ((HEAD, ROWS), F32)],
        [((ROWS, HEAD), BF16), ((PROMPT + 2 * CHUNK, ROWS), F32)],
        2,
        PROMPT + 2 * CHUNK,
    )
    out, pgrad, dq_prompt, cols, delta, peak = call(
        middle_kernel,
        [place],
        [queries, cotangent, pkv, rkv[1], rkv[2]] + list(forward),
        [((BLOCK, ROWS), BF16), ((PROMPT, WIDE), BF16), ((HEAD, ROWS), F32), ((HEAD, ROWS), BF16),
         ((1, ROWS), F32), ((1, ROWS), F32)],
        [((ROWS, HEAD), BF16), ((ROWS, HEAD), BF16), ((HEAD, ROWS), BF16), ((1, ROWS), F32),
         ((2 * CHUNK, ROWS), F32), ((8, ROWS), F32), ((8, ROWS), F32), ((HEAD, ROWS), F32)],
        6,
        PROMPT,
    )
    dq, rgrad = call(
        resp_backward_kernel,
        [place],
        [queries] + rkv + [cols, delta, peak, dq_prompt],
        [((BLOCK, ROWS), BF16), ((4, LEN // 4, WIDE), BF16)],
        [((ROWS, HEAD), BF16), ((ROWS, HEAD), BF16), ((HEAD, ROWS), F32)],
        5,
        LEN,
    )

    near, _ = lax.optimization_barrier((exchange(pgrad.reshape(8, PROMPT // 8, WIDE), NEAR), rgrad))
    part = lax.optimization_barrier(jnp.sum(near.astype(F32), 0)).astype(BF16)
    part = exchange(part.reshape(16, PIECE, WIDE), ("zh", "zl"))

    column = total_of([rgrad[0]] + [around_x(rgrad[k], k) for k in (1, 2, 3)])
    sent = column.astype(BF16)
    down = [along_zl(sent[k * BLOCK:(k + 1) * BLOCK], -k) for k in (1, 2, 3)]
    part, *down = lax.optimization_barrier((part, *down))
    grad_resp = total_of([column[:BLOCK]] + down)

    pieces = gather(total_of(part).astype(BF16), RESP, 16).reshape(4, 4, PIECE, WIDE)
    grad_prompt = total_of([pieces[:, x] for x in range(4)]).reshape(4 * PIECE, WIDE)
    return (
        out[None],
        dq[None],
        grad_resp[None, :, :HEAD],
        grad_resp[None, :, HEAD:],
        grad_prompt[:, :HEAD],
        grad_prompt[:, HEAD:],
    )


def solution(mesh):
    fine = jax.sharding.Mesh(mesh.devices.reshape(4, 4, 2, 4, 4), AXES)
    rows = P(CTX, RESP, None)
    return jax.shard_map(
        per_device,
        mesh=fine,
        in_specs=(rows, rows, rows, P(CTX, None), P(CTX, None), rows, P(CTX)),
        out_specs=(rows, rows, rows, rows, P(CTX, None), P(CTX, None)),
        check_vma=False,
    )
```
